256 devices in a mesh: row: 16 (over x, z_lo), col: 4 (over z_hi, core), hid: 4 (over y).
Axes of the slice: x: 4, y: 4, z: 8 (z_hi: 2, z_lo: 4; z = z_hi * 4 + z_lo), core: 2. Of those that a mesh axis runs over, the one named last changes fastest.
Arguments:
- features: bfloat16 [1024, 256, 512], P('hid', 'row', 'col'), may hold values from -6 to 6
- dw_kernel: float32 [1024, 7, 7], P('hid'), may hold values from -0.875 to 0.875
- dw_bias: float32 [1024], P('hid'), may hold values from -3 to 3
- norm_gain: float32 [1024], P('hid'), may hold values from 0.5 to 1.5
- norm_bias: float32 [1024], P('hid'), may hold values from -3 to 3
- w_in: bfloat16 [4096, 1024], P('hid'), may hold values from -0.1875 to 0.1875
- b_in: float32 [4096], P('hid'), may hold values from -3 to 3
- w_out: bfloat16 [4096, 1024], P('hid'), may hold values from -0.125 to 0.125
- b_out: float32 [1024], P('hid'), may hold values from -3 to 3
- layer_scale: float32 [1024], P('hid'), may hold values from 0.3 to 1.5
Outputs:
- block_out: bfloat16 [1024, 256, 512], P('hid', 'row', 'col')
The draws below stay inside these ranges and needn't reach their ends.
All inputs are finite; a program needn't handle non-finite values.
Results may differ from the reference program's by a relative error of at most 0.013.
Values may be sent and summed in bfloat16 or wider, within the bound.
No kernel may reach another device: no remote copies, remote signals or barrier semaphores. Data moves between devices by JAX's collectives and lax.ppermute only.
A program may use at most 128 MiB of HBM per device.

```python
import math
import jax
import jax.numpy as jnp
from jax import lax

C = 1024
FF = 4096
K = 7
H = 256
W = 512


def with_spikes(array, own_key, source, target, parts, factor):
    def block_of(position):
        return (jnp.arange(array.shape[position]) // (array.shape[position] // parts)).reshape((-1,) + (1,) * (array.ndim - 1 - position))

    first = jax.random.permutation(own_key, parts)[block_of(target)]
    second = (block_of(target) + parts // 2) % parts
    return jnp.where((block_of(source) == first) | (block_of(source) == second), factor * array, array)


def levels(own_key, shape, cuts, smallest, largest):
    loudness = 1.0
    for position, blocks in cuts:
        steps = jax.random.uniform(jax.random.fold_in(jax.random.fold_in(own_key, 6), position), (blocks,), jnp.float32, smallest / len(cuts), largest / len(cuts))
        loudness = loudness * jnp.repeat(jnp.exp(steps), shape[position] // blocks).reshape((-1,) + (1,) * (len(shape) - 1 - position))
    return loudness


def gaussian(own_key, extent, deviation, reach, shards=(), kind=jnp.bfloat16):
    array = deviation * jax.random.normal(own_key, extent, jnp.float32)
    if shards:
        array = array * levels(own_key, extent, shards, -0.22, 0.18)
    return jnp.clip(array, -reach, reach).astype(kind)


def gaussian_with(key, dims, scale, reach, split, heavy, held_as=jnp.bfloat16):
    values = scale * jax.random.normal(key, dims, jnp.float32)
    if split:
        values = values * levels(key, dims, split, -0.22, 0.18)
    return jnp.clip(with_spikes(values, jax.random.fold_in(key, 3), *heavy), -reach, reach).astype(held_as)


def setup_inputs(seed: int = 0) -> dict:
    splits = jax.random.split(jax.random.key(seed), 11)
    return {
        "features": gaussian(splits[0], (C, H, W), 1.0, 6.0, ((0, 4), (1, 16), (2, 4))),
        "dw_kernel": gaussian(splits[1], (C, K, K), 49 ** -0.5, 0.875, ((0, 4),), jnp.float32),
        "dw_bias": gaussian(splits[2], (C,), 0.5, 3.0, ((0, 4),), jnp.float32),
        "norm_gain": jnp.clip(1.0 + 0.1 * jax.random.normal(splits[3], (C,), jnp.float32), 0.5, 1.5),
        "norm_bias": gaussian(splits[4], (C,), 0.5, 3.0, ((0, 4),), jnp.float32),
        "w_in": gaussian(splits[5], (FF, C), C ** -0.5, 0.1875, ((0, 4),)),
        "b_in": gaussian(splits[6], (FF,), 0.5, 3.0, ((0, 4),), jnp.float32),
        "w_out": gaussian_with(splits[7], (FF, C), FF ** -0.5, 0.125, ((0, 4),), (0, 1, 4, 2.0)),
        "b_out": gaussian(splits[8], (C,), 0.5, 3.0, ((0, 4),), jnp.float32),
        "layer_scale": jnp.clip(jnp.exp(math.log(1.5) - 1.60943787 * jax.random.uniform(splits[9], (C,), jnp.float32) ** levels(splits[9], (C,), ((0, 4),), -0.2, 0.2)), 0.3, 1.5),
    }


def reference(features, dw_kernel, dw_bias, norm_gain, norm_bias, w_in, b_in, w_out, b_out, layer_scale):
    chans, rows, cols = features.shape
    padded = jnp.pad(features.astype(jnp.float32), ((0, 0), (3, 3), (3, 3)))
    mixed = jnp.zeros((chans, rows, cols), jnp.float32) + dw_bias[:, None, None]
    for a in range(7):
        for b in range(7):
            mixed = mixed + dw_kernel[:, a, b][:, None, None] * padded[:, a:a + rows, b:b + cols]
    mean = lax.optimization_barrier(jnp.sum(mixed, axis=0)) / chans
    var = lax.optimization_barrier(jnp.sum(mixed * mixed, axis=0)) / chans - mean * mean
    normed = ((mixed - mean) * lax.rsqrt(var + 1e-06) * norm_gain[:, None, None] + norm_bias[:, None, None]).astype(jnp.bfloat16)
    by_row = jnp.transpose(normed, (1, 0, 2))

    def one_row(slab):
        pre = lax.dot_general(w_in, slab, (((1,), (0,)), ((), ())), preferred_element_type=jnp.float32)
        hidden = jax.nn.gelu(pre + b_in[:, None], approximate=False).astype(jnp.bfloat16)
        return lax.dot_general(w_out, hidden, (((0,), (0,)), ((), ())), preferred_element_type=jnp.float32)
    mlp = jnp.transpose(lax.map(one_row, by_row), (1, 0, 2))
    result = features.astype(jnp.float32) + layer_scale[:, None, None] * (mlp + b_out[:, None, None])
    return result.astype(jnp.bfloat16)
```

```python
import functools
import jax
import jax.numpy as jnp
from jax import lax
from jax.experimental import pallas as pl
from jax.experimental.pallas import tpu as pltpu
from jax.sharding import PartitionSpec as P

F32 = jnp.float32
BF = jnp.bfloat16
VM = pl.BlockSpec(memory_space=pltpu.VMEM)
SM = pl.BlockSpec(memory_space=pltpu.SMEM)
HB = pl.BlockSpec(memory_space=pl.ANY)
NT = (((1,), (1,)), ((), ()))
CB = 32


def params(mib):
    return pltpu.CompilerParams(vmem_limit_bytes=mib << 20)


def turn_kernel(x_ref, xt_ref, l_ref, r_ref, xf):
    xf[...] = x_ref[...].astype(F32).reshape(4096, 128)
    for r in range(16):
        for h in range(2):
            t = xf[pl.ds(h * 2048 + r, 128, stride=16), :]
            xt_ref[r, :, h * 128 : (h + 1) * 128] = t.T.astype(BF)
    for j in range(3):
        l_ref[:, j * 256 : (j + 1) * 256] = xt_ref[:, j, :]
        r_ref[:, j * 256 : (j + 1) * 256] = xt_ref[:, 125 + j, :]


def turn(x):
    edge = jax.ShapeDtypeStruct((16, 768), BF)
    return pl.pallas_call(
        turn_kernel,
        out_shape=(jax.ShapeDtypeStruct((16, 128, 256), BF), edge, edge),
        in_specs=[VM],
        out_specs=(VM, VM, VM),
        scratch_shapes=[pltpu.VMEM((4096, 128), F32)],
        compiler_params=params(16),
        cost_estimate=pl.CostEstimate(flops=0, bytes_accessed=4 << 20, transcendentals=0),
        name="turn",
    )(x)


def conv_kernel(
    sc, xt_ref, l_ref, r_ref, top_ref, bot_ref, ct_ref, cb_ref, kw_ref, o0, o1, o2, o3, xs
):
    for h in range(2):
        hs = slice(h * 128, (h + 1) * 128)
        for r in range(16):
            xs[h, 3 + r, 8:136, :] = xt_ref[r, :, hs].astype(F32)
        for r in range(3):
            xs[h, r, 8:136, :] = top_ref[r, :, hs].astype(F32)
            xs[h, 19 + r, 8:136, :] = bot_ref[r, :, hs].astype(F32)
        for j in range(3):
            js = slice(j * 256 + h * 128, j * 256 + (h + 1) * 128)
            ks = slice(768 + j * 256 + h * 128, 768 + j * 256 + (h + 1) * 128)
            xs[h, 3:19, 5 + j, :] = l_ref[:, js].astype(F32)
            xs[h, 3:19, 136 + j, :] = r_ref[:, js].astype(F32)
            xs[h, 0:3, 5 + j, :] = ct_ref[:, js].astype(F32)
            xs[h, 0:3, 136 + j, :] = ct_ref[:, ks].astype(F32)
            xs[h, 19:22, 5 + j, :] = cb_ref[:, js].astype(F32)
            xs[h, 19:22, 136 + j, :] = cb_ref[:, ks].astype(F32)
    for k, o in enumerate((o0, o1, o2, o3)):
        row0 = 4 * lax.rem(sc[0] + k, 4)
        for h in range(2):
            hs = slice(h * 128, (h + 1) * 128)
            for c0 in range(0, 128, CB):
                acc = [jnp.zeros((CB, 128), F32) for _ in range(4)]
                for b in range(7):
                    for ri in range(10):
                        xv = xs[h, row0 + ri, c0 + 5 + b : c0 + 5 + b + CB, :]
                        for ro in range(4):
                            a = ri - ro
                            if 0 <= a < 7:
                                acc[ro] = acc[ro] + kw_ref[a * 7 + b : a * 7 + b + 1, hs] * xv
                for ro in range(4):
                    o[ro, c0 : c0 + CB, hs] = acc[ro].astype(BF)


def conv(sc, *args):
    o = jax.ShapeDtypeStruct((4, 128, 256), BF)
    return pl.pallas_call(
        conv_kernel,
        out_shape=(o,) * 4,
        in_specs=[SM] + [VM] * 8,
        out_specs=(VM,) * 4,
        scratch_shapes=[pltpu.VMEM((2, 22, 144, 128), F32)],
        compiler_params=params(16),
        cost_estimate=pl.CostEstimate(flops=60_000_000, bytes_accessed=4 << 20, transcendentals=0),
        name="conv",
    )(sc, *args)


def gelu(p):
    return 0.5 * p * (1.0 + lax.erf(p * 0.7071067811865476))


def mlp_kernel(sc, *refs):
    m = refs[0:4]
    pp = refs[4]
    w_in, w_out = refs[5:7]
    mine, other = refs[7:12], refs[12:17]
    outs = refs[17:21]
    n_ref, acc, win, wout, bv, sems = refs[21:27]
    y, core, c0, c1 = sc[0], sc[1], sc[2], sc[3]
    color_mine = jnp.where(core == 0, c0, c1)
    color_other = jnp.where(core == 0, c1, c0)
    copies = [[] for _ in range(5)]

    def load(chunk, src, dst):
        copy = pltpu.make_async_copy(src, dst, sems.at[sum(len(c) for c in copies)])
        copy.start()
        copies[chunk].append(copy)

    load(0, w_in, win.at[0:1024])
    load(0, w_out, wout.at[0:1024])
    for s, side in enumerate((mine, other)):
        for a in range(4):
            for k in range(3):
                base = 1024 + a * 768 + k * 256 + s * 128
                for w, dst in ((0, win), (1, wout)):
                    start = k * 256 + w * 128
                    if a < 3:
                        src = side[a].at[start : start + 128]
                    elif start < 384:
                        src = side[3].at[start : start + 128]
                    else:
                        src = side[4].at[start - 384 : start - 256]
                    load(1 + a, src, dst.at[base : base + 128])

    def wide(q, first, count):
        return jnp.concatenate([pp[q, first + i] for i in range(count)], axis=1)

    total = jnp.zeros((512, 1), F32)
    squares = jnp.zeros((512, 1), F32)
    for k in range(4):
        q = lax.rem(y + 4 - k, 4)
        v = m[k][...].astype(F32) + wide(q, 0, 2)
        total = total + jnp.sum(v, axis=1, keepdims=True)
        squares = squares + jnp.sum(v * v, axis=1, keepdims=True)
    mean = total * (1.0 / 1024)
    rstd = lax.rsqrt(squares * (1.0 / 1024) - mean * mean + 1e-06)
    for k in range(4):
        q = lax.rem(y + 4 - k, 4)
        v = m[k][...].astype(F32) + wide(q, 0, 2)
        v = (v - mean) * rstd * wide(q, 2, 2) + wide(q, 4, 2)
        n_ref[:, pl.ds(pl.multiple_of(q * 256, 256), 256)] = v.astype(BF)

    def block(first, size, bias, fresh):
        pre = lax.dot_general(
            n_ref[...], win[first : first + size], NT, preferred_element_type=F32
        )
        h = gelu(pre + bias).astype(BF)
        for q in range(4):
            part = jnp.dot(
                h,
                wout[first : first + size, q * 256 : (q + 1) * 256],
                preferred_element_type=F32,
            )
            acc[q] = part if fresh else acc[q] + part

    for copy in copies[0]:
        copy.wait()
    block(0, 1024, wide(y, 6, 8), True)
    for a, shift in enumerate((0, 1, 3, 2)):
        for k in range(3):
            row = lax.rem(y + 1 + k, 4)
            for s in range(2):
                color = lax.rem((color_other if s else color_mine) + shift, 4)
                half = (1 - core) if s else core
                bv[a, :, k * 256 + s * 128 : k * 256 + s * 128 + 128] = pp[
                    row, 6 + half * 4 + color
                ]
        for copy in copies[1 + a]:
            copy.wait()
        block(1024 + a * 768, 768, bv[a], False)
    for k in range(4):
        outs[k][...] = acc[lax.rem(y + k, 4)].astype(BF)


def mlp(sc, mixed, pp, w_in, w_out, mine, other):
    o = jax.ShapeDtypeStruct((512, 256), BF)
    return pl.pallas_call(
        mlp_kernel,
        out_shape=(o,) * 4,
        in_specs=[SM] + [VM] * 5 + [HB] * 12,
        out_specs=(VM,) * 4,
        scratch_shapes=[
            pltpu.VMEM((512, 1024), BF),
            pltpu.VMEM((4, 512, 256), F32),
            pltpu.VMEM((4096, 1024), BF),
            pltpu.VMEM((4096, 1024), BF),
            pltpu.VMEM((4, 1, 768), F32),
            pltpu.SemaphoreType.DMA((50,)),
        ],
        compiler_params=params(48),
        cost_estimate=pl.CostEstimate(
            flops=8_600_000_000, bytes_accessed=20 << 20, transcendentals=2 << 20
        ),
        name="mlp",
    )(sc, *mixed, pp, w_in, w_out, *mine, *other)


def final_kernel(sc, x_ref, ls_ref, bo_ref, f0, f1, f2, f3, o_ref, t):
    for k, f in enumerate((f0, f1, f2, f3)):
        row0 = 4 * lax.rem(sc[0] + 4 - k, 4)
        for i in range(4):
            v = f[i * 128 : (i + 1) * 128, :].astype(F32)
            v = ls_ref[...] * (v + bo_ref[...])
            for h in range(2):
                t[pl.ds(h * 2048 + row0 + i, 128, stride=16), :] = v[
                    :, h * 128 : (h + 1) * 128
                ].T
    o_ref[...] = (x_ref[...].astype(F32) + t[...].reshape(256, 16, 128)).astype(BF)


def final(sc, x, ls, bo, parts):
    return pl.pallas_call(
        final_kernel,
        out_shape=jax.ShapeDtypeStruct((256, 16, 128), BF),
        in_specs=[SM] + [VM] * 7,
        out_specs=VM,
        scratch_shapes=[pltpu.VMEM((4096, 128), F32)],
        compiler_params=params(16),
        cost_estimate=pl.CostEstimate(flops=1 << 20, bytes_accessed=4 << 20, transcendentals=0),
        name="final",
    )(sc, x, ls, bo, *parts)


def from_hid(x, k):
    return lax.ppermute(x, "hid", [((i + k) % 4, i) for i in range(4)])


def to_hid(x, k):
    return lax.ppermute(x, "hid", [(i, (i + k) % 4) for i in range(4)])


def place(x, z, core):
    return (x * 4 + z % 4) * 4 + (z // 4) * 2 + core


def from_plane(v, step, major):
    pairs = []
    for x in range(4):
        for z in range(8):
            for core in range(2):
                along_x = (core == 0) == major
                sx, sz = ((x + step) % 4, z) if along_x else (x, (z + step) % 8)
                pairs.append((place(sx, sz, core), place(x, z, core)))
    return lax.ppermute(v, ("row", "col"), pairs)


def from_core(v):
    return lax.ppermute(v, "col", [(0, 1), (1, 0), (2, 3), (3, 2)])


def shift(v, axis, up):
    n = lax.axis_size(axis)
    pairs = [(i, i + 1) for i in range(n - 1)]
    return lax.ppermute(v, axis, pairs if up else [(b, a) for a, b in pairs])


def on_device(
    features, dw_kernel, dw_bias, norm_gain, norm_bias, w_in, b_in, w_out, b_out, layer_scale
):
    row, col, y = lax.axis_index("row"), lax.axis_index("col"), lax.axis_index("hid")
    x, zl, core = row // 4, row % 4, col % 2
    c0, c1 = (x + 2 * zl) % 4, (2 * x + zl) % 4
    color = jnp.where(core == 0, c0, c1)
    sc = jnp.stack([y, core, c0, c1]).astype(jnp.int32)

    pp = lax.all_gather(
        jnp.concatenate([dw_bias, norm_gain, norm_bias, b_in]).reshape(14, 1, 128), "hid"
    )

    xt, left, right = turn(features)
    halo_l = shift(right, "col", True)
    halo_r = shift(left, "col", False)
    top = shift(xt[13:16], "row", True)
    bot = shift(xt[0:3], "row", False)
    corner_t = shift(jnp.concatenate([halo_l[13:16], halo_r[13:16]], 1), "row", True)
    corner_b = shift(jnp.concatenate([halo_l[0:3], halo_r[0:3]], 1), "row", False)

    start = 512 * core + 128 * color
    piece = jnp.concatenate(
        [
            lax.dynamic_slice_in_dim(w_in, start, 128, 0),
            lax.dynamic_slice_in_dim(w_out, start, 128, 0),
        ]
    )
    held = jnp.concatenate([from_hid(piece, k) for k in (1, 2, 3)])
    mine = [
        held,
        from_plane(held, 1, True),
        from_plane(held, -1, True),
        from_plane(held[:384], 1, False),
        from_plane(held[384:], -1, False),
    ]
    other = [from_core(v) for v in mine]

    kw = jnp.transpose(dw_kernel.reshape(256, 49))
    mixed = conv(sc, xt, halo_l, halo_r, top, bot, corner_t, corner_b, kw)
    mixed = [mixed[0]] + [to_hid(mixed[k], k) for k in (1, 2, 3)]
    mixed = [v.reshape(512, 256) for v in mixed]
    parts = mlp(sc, mixed, pp, w_in, w_out, mine, other)
    parts = [parts[0]] + [to_hid(parts[k], k) for k in (1, 2, 3)]
    return final(sc, features, layer_scale[None, :], b_out[None, :], parts)


def solution(mesh):
    return jax.shard_map(
        on_device,
        mesh=mesh,
        in_specs=(
            P("hid", "row", "col"),
            P("hid", None, None),
            P("hid"),
            P("hid"),
            P("hid"),
            P("hid", None),
            P("hid"),
            P("hid", None),
            P("hid"),
            P("hid"),
        ),
        out_specs=P("hid", "row", "col"),
        check_vma=False,
    )
```

```python
import functools
import jax
import jax.numpy as jnp
from jax import lax
from jax.experimental import pallas as pl
from jax.experimental.pallas import tpu as pltpu
from jax.sharding import PartitionSpec as P

F32 = jnp.float32
BF = jnp.bfloat16
VM = pl.BlockSpec(memory_space=pltpu.VMEM)
SM = pl.BlockSpec(memory_space=pltpu.SMEM)
HB = pl.BlockSpec(memory_space=pl.ANY)
NT = (((1,), (1,)), ((), ()))
CB = 32


def params(mib):
    return pltpu.CompilerParams(vmem_limit_bytes=mib << 20)


def turn_kernel(sc, x_ref, xt_ref, a_ref, b_ref, xf):
    xf[...] = x_ref[...].astype(F32).reshape(4096, 128)
    for r in range(16):
        for h in range(2):
            t = xf[pl.ds(h * 2048 + r, 128, stride=16), :]
            xt_ref[r, :, h * 128 : (h + 1) * 128] = t.T.astype(BF)
    for j in range(3):
        js = slice(j * 256, (j + 1) * 256)
        low, high = xt_ref[:, j, :].astype(F32), xt_ref[:, 125 + j, :].astype(F32)
        a_ref[:, js] = jnp.where(sc[1] == 0, high, low).astype(BF)
        b_ref[:, js] = jnp.where(sc[1] == 0, low, high).astype(BF)


def turn(sc, x):
    edge = jax.ShapeDtypeStruct((16, 768), BF)
    return pl.pallas_call(
        turn_kernel,
        out_shape=(jax.ShapeDtypeStruct((16, 128, 256), BF), edge, edge),
        in_specs=[SM, VM],
        out_specs=(VM, VM, VM),
        scratch_shapes=[pltpu.VMEM((4096, 128), F32)],
        compiler_params=params(16),
        cost_estimate=pl.CostEstimate(flops=0, bytes_accessed=4 << 20, transcendentals=0),
        name="turn",
    )(sc, x)


def pack_kernel(xt_ref, a_ref, b_ref, r1_ref, r3_ref, down_ref, up_ref, relay_up, relay_down):
    for r in range(3):
        down_ref[r * 128 : (r + 1) * 128, :] = xt_ref[13 + r]
        up_ref[r * 128 : (r + 1) * 128, :] = xt_ref[r]
    edges = [
        edge[:, j * 256 : (j + 1) * 256].astype(F32) for edge in (a_ref, b_ref) for j in range(3)
    ]
    none = jnp.zeros((8, 256), F32)
    down_ref[384:416, :] = jnp.concatenate([v[12:16] for v in edges] + [none]).astype(BF)
    up_ref[384:416, :] = jnp.concatenate([v[0:4] for v in edges] + [none]).astype(BF)
    relay_up[...] = r1_ref[0:128, :]
    relay_down[...] = r3_ref[128:256, :]


def pack(xt, a, b, r1, r3):
    o = jax.ShapeDtypeStruct((416, 256), BF)
    w = jax.ShapeDtypeStruct((128, 1024), BF)
    return pl.pallas_call(
        pack_kernel,
        out_shape=(o, o, w, w),
        in_specs=[VM] * 5,
        out_specs=(VM,) * 4,
        compiler_params=params(16),
        cost_estimate=pl.CostEstimate(flops=0, bytes_accessed=2 << 20, transcendentals=0),
        name="pack",
    )(xt, a, b, r1, r3)


def cut_kernel(sc, w_in, w_out, piece, sems):
    start = pl.multiple_of(sc[8], 128)
    copies = [
        pltpu.make_async_copy(w.at[pl.ds(start, 128)], piece.at[128 * i : 128 * i + 128], sems.at[i])
        for i, w in enumerate((w_in, w_out))
    ]
    for copy in copies:
        copy.start()
    for copy in copies:
        copy.wait()


def cut(sc, w_in, w_out):
    return pl.pallas_call(
        cut_kernel,
        out_shape=jax.ShapeDtypeStruct((256, 1024), BF),
        in_specs=[SM, HB, HB],
        out_specs=VM,
        scratch_shapes=[pltpu.SemaphoreType.DMA((2,))],
        compiler_params=params(60),
        cost_estimate=pl.CostEstimate(flops=0, bytes_accessed=1 << 20, transcendentals=0),
        name="cut",
    )(sc, w_in, w_out)


def taps(sc, xs, kw_ref, edge, sums, outs):
    @pl.loop(0, 8)
    def _(step):
        h, k = lax.rem(step, 2), step // 2
        q = lax.rem(sc[0] + k, 4)
        row0 = 2 * q + 6 * (q // 2) if edge else 2 * q
        for c0 in range(0, 128, CB):
            acc = [jnp.zeros((CB, 128), F32) for _ in range(2)]
            for b in range(7):
                for ri in range(8):
                    xv = xs[h, row0 + ri, c0 + 5 + b : c0 + 5 + b + CB, :]
                    for ro in range(2):
                        a = ri - ro
                        if 0 <= a < 7:
                            acc[ro] = acc[ro] + kw_ref[h, a * 7 + b : a * 7 + b + 1, :] * xv
            for ro in range(2):
                sums[k, h, ro * 128 + c0 : ro * 128 + c0 + CB, :] = acc[ro].astype(BF)

    for k, o in enumerate(outs):
        for h in range(2):
            o[0:256, h * 128 : (h + 1) * 128] = sums[k, h]


def columns(sc, a, b):
    a, b, first = a.astype(F32), b.astype(F32), sc[1] == 0
    low = jnp.where(sc[6] > 0, jnp.where(first, b, a), 0.0)
    high = jnp.where(sc[7] > 0, jnp.where(first, a, b), 0.0)
    return low, high


def inner_kernel(sc, xt_ref, a_ref, b_ref, kw_ref, o0, o1, o2, o3, xs, sums):
    for h in range(2):
        hs = slice(h * 128, (h + 1) * 128)
        for r in range(14):
            xs[h, r, 8:136, :] = xt_ref[1 + r, :, hs].astype(F32)
        for j in range(3):
            js = slice(j * 256 + h * 128, j * 256 + (h + 1) * 128)
            low, high = columns(sc, a_ref[:, js], b_ref[:, js])
            xs[h, :, 5 + j, :] = low[1:15]
            xs[h, :, 136 + j, :] = high[1:15]
    taps(sc, xs, kw_ref, False, sums, (o0, o1, o2, o3))


def edge_kernel(
    sc, xt_ref, a_ref, b_ref, top_ref, bot_ref, kw_ref, p_ref, o0, o1, o2, o3, xs, sums
):
    up, down = sc[4] > 0, sc[5] > 0
    for h in range(2):
        hs = slice(h * 128, (h + 1) * 128)
        for r in range(7):
            xs[h, 3 + r, 8:136, :] = xt_ref[r, :, hs].astype(F32)
            xs[h, 10 + r, 8:136, :] = xt_ref[9 + r, :, hs].astype(F32)
        for r in range(3):
            rs = slice(r * 128, (r + 1) * 128)
            xs[h, r, 8:136, :] = jnp.where(up, top_ref[rs, hs].astype(F32), 0.0)
            xs[h, 17 + r, 8:136, :] = jnp.where(down, bot_ref[rs, hs].astype(F32), 0.0)
        tc, bc = top_ref[384:416, hs].astype(F32), bot_ref[384:416, hs].astype(F32)
        for j in range(3):
            js = slice(j * 256 + h * 128, j * 256 + (h + 1) * 128)
            sides = columns(sc, a_ref[:, js], b_ref[:, js])
            ra, rb = slice(4 * j, 4 * j + 4), slice(12 + 4 * j, 16 + 4 * j)
            tops = columns(sc, tc[ra], tc[rb])
            bots = columns(sc, bc[ra], bc[rb])
            for at, v, t, d in zip((5 + j, 136 + j), sides, tops, bots):
                xs[h, 3:10, at, :] = v[0:7]
                xs[h, 10:17, at, :] = v[9:16]
                xs[h, 0:3, at, :] = jnp.where(up, t, 0.0)[1:4]
                xs[h, 17:20, at, :] = jnp.where(down, d, 0.0)[0:3]
    for o in (o0, o1, o2, o3):
        o[256:288] = p_ref[...]
    taps(sc, xs, kw_ref, True, sums, (o0, o1, o2, o3))


def conv_inner(sc, *args):
    o = jax.ShapeDtypeStruct((256, 256), BF)
    return pl.pallas_call(
        inner_kernel,
        out_shape=(o,) * 4,
        in_specs=[SM] + [VM] * 4,
        out_specs=(VM,) * 4,
        scratch_shapes=[pltpu.VMEM((2, 14, 144, 128), F32), pltpu.VMEM((4, 2, 256, 128), BF)],
        compiler_params=params(16),
        cost_estimate=pl.CostEstimate(flops=30_000_000, bytes_accessed=4 << 20, transcendentals=0),
        name="conv_inner",
    )(sc, *args)


def conv_edge(sc, *args):
    o = jax.ShapeDtypeStruct((288, 256), BF)
    return pl.pallas_call(
        edge_kernel,
        out_shape=(o,) * 4,
        in_specs=[SM] + [VM] * 7,
        out_specs=(VM,) * 4,
        scratch_shapes=[pltpu.VMEM((2, 20, 144, 128), F32), pltpu.VMEM((4, 2, 256, 128), BF)],
        compiler_params=params(16),
        cost_estimate=pl.CostEstimate(flops=30_000_000, bytes_accessed=4 << 20, transcendentals=0),
        name="conv_edge",
    )(sc, *args)


def gelu(p):
    return 0.5 * p * (1.0 + lax.erf(p * 0.7071067811865476))


def norm_kernel(sc, i0, i1, i2, i3, e0, e1, e2, e3, n_ref, bias):
    sides = []
    for k, (inner, edge) in enumerate(((i0, e0), (i1, e1), (i2, e2), (i3, e3))):
        p = sum(edge[256 + 8 * t : 264 + 8 * t, :].astype(F32) for t in (2, 1, 0))
        for i in range(8):
            bias[(4 - k) % 4, i] = p[3 + i // 2 : 4 + i // 2, i % 2 * 128 : i % 2 * 128 + 128]
        sides.append((inner, edge, p))
    for part in range(2):
        @pl.loop(0, 2)
        def _(step):
            rows = pl.ds(pl.multiple_of(step * 128, 128), 128)
            total = jnp.zeros((128, 1), F32)
            squares = jnp.zeros((128, 1), F32)
            for *m, p in sides:
                v = m[part][rows, :].astype(F32) + p[0:1]
                total = total + jnp.sum(v, axis=1, keepdims=True)
                squares = squares + jnp.sum(v * v, axis=1, keepdims=True)
            mean = total * (1.0 / 1024)
            rstd = lax.rsqrt(squares * (1.0 / 1024) - mean * mean + 1e-06)
            at = pl.ds(pl.multiple_of(256 * part + step * 128, 128), 128)
            for k, (*m, p) in enumerate(sides):
                q = lax.rem(sc[0] + 4 - k, 4)
                v = m[part][rows, :].astype(F32) + p[0:1]
                v = (v - mean) * rstd * p[1:2] + p[2:3]
                n_ref[at, pl.ds(pl.multiple_of(q * 256, 256), 256)] = v.astype(BF)


def norm(sc, inner, edge):
    return pl.pallas_call(
        norm_kernel,
        out_shape=(
            jax.ShapeDtypeStruct((512, 1024), BF),
            jax.ShapeDtypeStruct((4, 8, 1, 128), F32),
        ),
        in_specs=[SM] + [VM] * 8,
        out_specs=(VM, VM),
        compiler_params=params(16),
        cost_estimate=pl.CostEstimate(flops=1 << 23, bytes_accessed=2 << 20, transcendentals=0),
        name="norm",
    )(sc, *inner, *edge)


def blocks(pixels, acc, at, items, out):
    items = [(win, wout, jnp.concatenate(bias, axis=1)) for win, wout, bias in items]

    @pl.loop(0, 2 * len(pixels))
    def _(step):
        rows = pl.ds(pl.multiple_of(lax.rem(step, 2) * 256, 256), 256)
        n = pixels[0][rows, :]
        if len(pixels) > 1:
            n = jnp.where(step < 2, n, pixels[1][rows, :])
        total = None
        for win, wout, bias in items:
            pre = lax.dot_general(n, win[...], NT, preferred_element_type=F32)
            h = gelu(pre + bias).astype(BF)
            part = jnp.dot(h, wout[...], preferred_element_type=F32)
            total = part if total is None else total + part
        here = pl.ds(pl.multiple_of(step * 256, 256), 256)
        there = pl.ds(pl.multiple_of(at + step * 256, 256), 256)
        for q in range(4):
            part = total[:, q * 256 : (q + 1) * 256]
            if acc is not None:
                part = part + acc[q, there, :]
            out[q, here, :] = part.astype(out.dtype)


def shards_bias(sc, bias, shift):
    color = jnp.where(sc[1] == 0, sc[2], sc[3])
    return [bias[k, sc[1] * 4 + lax.rem(color + shift, 4)] for k in (1, 2, 3)]


def first_kernel(sc, n_ref, n_other, bias, w_in, w_out, held, out):
    own = pl.ds(pl.multiple_of(sc[1] * 512, 512), 512)
    values = [bias[0, sc[1] * 4 + c] for c in range(4)]
    items = [(w_in.at[own], w_out.at[own], values)]
    items += [(held.at[0:384], held.at[384:768], shards_bias(sc, bias, 0))]
    blocks((n_ref, n_other), None, 0, items, out)


def middle_kernel(sc, n_ref, n_other, bias, acc, plus, minus, out):
    items = [
        (w.at[0:384], w.at[384:768], shards_bias(sc, bias, shift))
        for w, shift in ((plus, 1), (minus, 3))
    ]
    blocks((n_ref, n_other), acc, 0, items, out)


def last_kernel(at, sc, n_ref, bias, acc, low, high, out):
    blocks((n_ref,), acc, at, [(low, high, shards_bias(sc, bias, 2))], out)


def mlp(kernel, sc, arrays, size, rows, out, name):
    return pl.pallas_call(
        kernel,
        out_shape=jax.ShapeDtypeStruct((4, rows, 256), out),
        in_specs=[SM] + [VM] * len(arrays),
        out_specs=VM,
        compiler_params=params(20),
        cost_estimate=pl.CostEstimate(
            flops=4_000 * size * rows, bytes_accessed=6 << 20, transcendentals=size * rows
        ),
        name=name,
    )(sc, *arrays)


def add_kernel(sc, acc, other, o0, o1, o2, o3):
    for k, o in enumerate((o0, o1, o2, o3)):
        q = lax.rem(sc[0] + k, 4)
        o[...] = (acc[q] + other[q].astype(F32)).astype(BF)


def add(sc, acc, other):
    return pl.pallas_call(
        add_kernel,
        out_shape=(jax.ShapeDtypeStruct((512, 256), BF),) * 4,
        in_specs=[SM, VM, VM],
        out_specs=(VM,) * 4,
        compiler_params=params(16),
        cost_estimate=pl.CostEstimate(flops=1 << 20, bytes_accessed=4 << 20, transcendentals=0),
        name="add",
    )(sc, acc, other)


def join_kernel(r1, ra, rb, r3, held, low, high, sems):
    moves = [(r1.at[0:128], 0), (ra, 128), (r3.at[0:128], 256)]
    moves += [(r1.at[128:256], 384), (rb, 512), (r3.at[128:256], 640)]
    copies = []
    for i, (src, at) in enumerate(moves):
        half, base = (low, at) if at < 384 else (high, at - 384)
        copies.append(pltpu.make_async_copy(src, held.at[at : at + 128], sems.at[2 * i]))
        copies.append(pltpu.make_async_copy(src, half.at[base : base + 128], sems.at[2 * i + 1]))
    for copy in copies:
        copy.start()
    for copy in copies:
        copy.wait()


def join(*pieces):
    half = jax.ShapeDtypeStruct((384, 1024), BF)
    return pl.pallas_call(
        join_kernel,
        out_shape=(jax.ShapeDtypeStruct((768, 1024), BF), half, half),
        in_specs=[HB] * 4,
        out_specs=(HB,) * 3,
        scratch_shapes=[pltpu.SemaphoreType.DMA((12,))],
        compiler_params=params(16),
        cost_estimate=pl.CostEstimate(flops=0, bytes_accessed=6 << 20, transcendentals=0),
        name="join",
    )(*pieces)


def final_kernel(sc, x_ref, ls_ref, bo_ref, f0, f1, f2, f3, o_ref, t):
    for k, f in enumerate((f0, f1, f2, f3)):
        q = lax.rem(sc[0] + 4 - k, 4)
        inner, edge = 4 + 2 * q, 2 * q + 8 * (q // 2)
        for i in range(4):
            row = inner + i if i < 2 else edge + i - 2
            v = f[i * 128 : (i + 1) * 128, :].astype(F32)
            v = ls_ref[...] * (v + bo_ref[...])
            for h in range(2):
                t[pl.ds(h * 2048 + row, 128, stride=16), :] = v[
                    :, h * 128 : (h + 1) * 128
                ].T
    o_ref[...] = (x_ref[...].astype(F32) + t[...].reshape(256, 16, 128)).astype(BF)


def final(sc, x, ls, bo, parts):
    return pl.pallas_call(
        final_kernel,
        out_shape=jax.ShapeDtypeStruct((256, 16, 128), BF),
        in_specs=[SM] + [VM] * 7,
        out_specs=VM,
        scratch_shapes=[pltpu.VMEM((4096, 128), F32)],
        compiler_params=params(16),
        cost_estimate=pl.CostEstimate(flops=1 << 20, bytes_accessed=4 << 20, transcendentals=0),
        name="final",
    )(sc, x, ls, bo, *parts)


def from_hid(x, k):
    return lax.ppermute(x, "hid", [((i + k) % 4, i) for i in range(4)])


def to_hid(x, k):
    return lax.ppermute(x, "hid", [(i, (i + k) % 4) for i in range(4)])


def place(x, z, core):
    return (x * 4 + z % 4) * 4 + (z // 4) * 2 + core


def from_plane(v, step, major):
    pairs = []
    for x in range(4):
        for z in range(8):
            for core in range(2):
                along_x = (core == 0) == major
                sx, sz = ((x + step) % 4, z) if along_x else (x, (z + step) % 8)
                pairs.append((place(sx, sz, core), place(x, z, core)))
    return lax.ppermute(v, ("row", "col"), pairs)


def from_core(v):
    return lax.ppermute(v, "col", [(0, 1), (1, 0), (2, 3), (3, 2)])


def around(v, up):
    return lax.ppermute(v, "row", [(i, (i + (1 if up else -1)) % 16) for i in range(16)])


def from_chip(v):
    return lax.ppermute(v, "col", [(1, 2), (2, 1), (0, 3), (3, 0)])


def after(values, *others):
    values = tuple(values)
    return lax.optimization_barrier(values + others)[: len(values)]


def on_device(
    features, dw_kernel, dw_bias, norm_gain, norm_bias, w_in, b_in, w_out, b_out, layer_scale
):
    row, col, y = lax.axis_index("row"), lax.axis_index("col"), lax.axis_index("hid")
    x, zl, core = row // 4, row % 4, col % 2
    c0, c1 = (x + 2 * zl) % 4, (2 * x + zl) % 4
    color = jnp.where(core == 0, c0, c1)
    start = 512 * core + 128 * color
    sc = jnp.stack([y, core, c0, c1, row, 15 - row, col, 3 - col, start]).astype(jnp.int32)

    piece = cut(sc, w_in, w_out)
    r1, r3 = from_hid(piece, 1), from_hid(piece, 3)

    xt, send_a, send_b = turn(sc, features)
    a, b = from_core(send_a), from_chip(send_b)
    kw = jnp.transpose(dw_kernel.reshape(2, 128, 49), (0, 2, 1))
    small = jnp.concatenate([dw_bias, norm_gain, norm_bias, b_in]).reshape(7, 256)
    small = jnp.pad(small, ((0, 1), (0, 0)))
    high = lax.reduce_precision(small, 8, 7)
    middle = lax.reduce_precision(small - high, 8, 7)
    lowest = small - high - middle
    small = jnp.concatenate([high, middle, lowest, jnp.zeros_like(high)]).astype(BF)
    b, kw, small = after([b, kw, small])
    down, up, ra, rb = pack(xt, a, b, r1, r3)
    top, bot = around(down, True), around(up, False)
    ra, rb = from_hid(ra, 1), from_hid(rb, 3)

    inner = conv_inner(sc, xt, a, b, kw)
    inner = [inner[0]] + [to_hid(inner[k], k) for k in (1, 2, 3)]
    held, low, high = join(r1, ra, rb, r3)
    plane = [
        from_plane(held, 1, True),
        from_plane(held, -1, True),
        from_plane(low, 1, False),
        from_plane(high, -1, False),
    ]
    top, bot = after([top, bot], held)
    edge = conv_edge(sc, xt, a, b, top, bot, kw, small)
    edge = [edge[0]] + [to_hid(edge[k], k) for k in (1, 2, 3)]

    n, bias = norm(sc, inner, edge)
    n_other = from_core(n)
    plus, minus, low, high = plane
    acc = mlp(first_kernel, sc, [n, n_other, bias, w_in, w_out, held], 896, 1024, F32, "mlp_first")
    plus, minus, acc = after([plus, minus, acc])
    acc = mlp(middle_kernel, sc, [n, n_other, bias, acc, plus, minus], 768, 1024, F32, "mlp_mid")
    low, high, acc = after([low, high, acc])
    last = functools.partial(last_kernel, 512)
    other = mlp(last, sc, [n_other, bias, acc, low, high], 384, 512, BF, "mlp_last_other")
    back = from_core(other)
    (acc,) = after([acc], other)
    last = functools.partial(last_kernel, 0)
    acc = mlp(last, sc, [n, bias, acc, low, high], 384, 512, F32, "mlp_last")
    parts = add(sc, acc, back)
    parts = [parts[0]] + [to_hid(parts[k], k) for k in (1, 2, 3)]
    return final(sc, features, layer_scale[None, :], b_out[None, :], parts)


def solution(mesh):
    return jax.shard_map(
        on_device,
        mesh=mesh,
        in_specs=(
            P("hid", "row", "col"),
            P("hid", None, None),
            P("hid"),
            P("hid"),
            P("hid"),
            P("hid", None),
            P("hid"),
            P("hid", None),
            P("hid"),
            P("hid"),
        ),
        out_specs=P("hid", "row", "col"),
        check_vma=False,
    )
```

```python
import functools
import jax
import jax.numpy as jnp
from jax import lax
from jax.experimental import pallas as pl
from jax.experimental.pallas import tpu as pltpu
from jax.sharding import PartitionSpec as P

F32 = jnp.float32
BF = jnp.bfloat16
VM = pl.BlockSpec(memory_space=pltpu.VMEM)
SM = pl.BlockSpec(memory_space=pltpu.SMEM)
HB = pl.BlockSpec(memory_space=pl.ANY)
NT = (((1,), (1,)), ((), ()))
CB = 32


def params(mib):
    return pltpu.CompilerParams(vmem_limit_bytes=mib << 20)


def turn_kernel(sc, x_ref, xt_ref, a_ref, b_ref, xf):
    xf.reshape(256, 24, 128)[:, 0:16, :] = x_ref[...].astype(F32)
    for r in range(16):
        for h in range(2):
            t = xf[pl.ds(h * 3072 + r, 128, stride=24), :]
            xt_ref[r, :, h * 128 : (h + 1) * 128] = t.T.astype(BF)
    for j in range(3):
        js = slice(j * 256, (j + 1) * 256)
        low, high = xt_ref[:, j, :].astype(F32), xt_ref[:, 125 + j, :].astype(F32)
        a_ref[:, js] = jnp.where(sc[1] == 0, high, low).astype(BF)
        b_ref[:, js] = jnp.where(sc[1] == 0, low, high).astype(BF)


def turn(sc, x):
    edge = jax.ShapeDtypeStruct((16, 768), BF)
    return pl.pallas_call(
        turn_kernel,
        out_shape=(jax.ShapeDtypeStruct((16, 128, 256), BF), edge, edge),
        in_specs=[SM, VM],
        out_specs=(VM, VM, VM),
        scratch_shapes=[pltpu.VMEM((6144, 128), F32)],
        compiler_params=params(16),
        cost_estimate=pl.CostEstimate(flops=0, bytes_accessed=4 << 20, transcendentals=0),
        name="turn",
    )(sc, x)


def pack_kernel(xt_ref, a_ref, b_ref, r1_ref, r3_ref, down_ref, up_ref, relay_up, relay_down):
    for r in range(3):
        down_ref[r * 128 : (r + 1) * 128, :] = xt_ref[13 + r]
        up_ref[r * 128 : (r + 1) * 128, :] = xt_ref[r]
    edges = [
        edge[:, j * 256 : (j + 1) * 256].astype(F32) for edge in (a_ref, b_ref) for j in range(3)
    ]
    none = jnp.zeros((8, 256), F32)
    down_ref[384:416, :] = jnp.concatenate([v[12:16] for v in edges] + [none]).astype(BF)
    up_ref[384:416, :] = jnp.concatenate([v[0:4] for v in edges] + [none]).astype(BF)
    relay_up[...] = r1_ref[0:128, :]
    relay_down[...] = r3_ref[128:256, :]


def pack(xt, a, b, r1, r3):
    o = jax.ShapeDtypeStruct((416, 256), BF)
    w = jax.ShapeDtypeStruct((128, 1024), BF)
    return pl.pallas_call(
        pack_kernel,
        out_shape=(o, o, w, w),
        in_specs=[VM] * 5,
        out_specs=(VM,) * 4,
        compiler_params=params(16),
        cost_estimate=pl.CostEstimate(flops=0, bytes_accessed=2 << 20, transcendentals=0),
        name="pack",
    )(xt, a, b, r1, r3)


def taps(sc, xs, kw_ref, edge, sums, outs):
    @pl.loop(0, 4)
    def _(step):
        h, g = lax.rem(step, 2), step // 2
        row0 = (10 if edge else 4) * g
        for c0 in range(0, 128, CB):
            acc = [jnp.zeros((CB, 128), F32) for _ in range(4)]
            for b in range(7):
                for ri in range(10):
                    xv = xs[h, row0 + ri, c0 + 5 + b : c0 + 5 + b + CB, :]
                    for ro in range(4):
                        a = ri - ro
                        if 0 <= a < 7:
                            acc[ro] = acc[ro] + kw_ref[h, a * 7 + b : a * 7 + b + 1, :] * xv
            for ro in range(4):
                at = ro % 2 * 128 + c0
                sums[2 * g + ro // 2, h, at : at + CB, :] = acc[ro].astype(BF)

    for k, o in enumerate(outs):
        q = lax.rem(sc[0] + k, 4)
        for h in range(2):
            o[0:256, h * 128 : (h + 1) * 128] = sums[q, h]


def columns(sc, a, b):
    a, b, first = a.astype(F32), b.astype(F32), sc[1] == 0
    low = jnp.where(sc[6] > 0, jnp.where(first, b, a), 0.0)
    high = jnp.where(sc[7] > 0, jnp.where(first, a, b), 0.0)
    return low, high


def inner_kernel(sc, xt_ref, a_ref, b_ref, kw_ref, o0, o1, o2, o3, xs, sums):
    for h in range(2):
        hs = slice(h * 128, (h + 1) * 128)
        for r in range(14):
            xs[h, r, 8:136, :] = xt_ref[1 + r, :, hs].astype(F32)
        for j in range(3):
            js = slice(j * 256 + h * 128, j * 256 + (h + 1) * 128)
            low, high = columns(sc, a_ref[:, js], b_ref[:, js])
            xs[h, :, 5 + j, :] = low[1:15]
            xs[h, :, 136 + j, :] = high[1:15]
    taps(sc, xs, kw_ref, False, sums, (o0, o1, o2, o3))


def edge_kernel(
    sc, xt_ref, a_ref, b_ref, top_ref, bot_ref, kw_ref, p_ref, o0, o1, o2, o3, xs, sums
):
    up, down = sc[4] > 0, sc[5] > 0
    for h in range(2):
        hs = slice(h * 128, (h + 1) * 128)
        for r in range(7):
            xs[h, 3 + r, 8:136, :] = xt_ref[r, :, hs].astype(F32)
            xs[h, 10 + r, 8:136, :] = xt_ref[9 + r, :, hs].astype(F32)
        for r in range(3):
            rs = slice(r * 128, (r + 1) * 128)
            xs[h, r, 8:136, :] = jnp.where(up, top_ref[rs, hs].astype(F32), 0.0)
            xs[h, 17 + r, 8:136, :] = jnp.where(down, bot_ref[rs, hs].astype(F32), 0.0)
        tc, bc = top_ref[384:416, hs].astype(F32), bot_ref[384:416, hs].astype(F32)
        for j in range(3):
            js = slice(j * 256 + h * 128, j * 256 + (h + 1) * 128)
            sides = columns(sc, a_ref[:, js], b_ref[:, js])
            ra, rb = slice(4 * j, 4 * j + 4), slice(12 + 4 * j, 16 + 4 * j)
            tops = columns(sc, tc[ra], tc[rb])
            bots = columns(sc, bc[ra], bc[rb])
            for at, v, t, d in zip((5 + j, 136 + j), sides, tops, bots):
                xs[h, 3:10, at, :] = v[0:7]
                xs[h, 10:17, at, :] = v[9:16]
                xs[h, 0:3, at, :] = jnp.where(up, t, 0.0)[1:4]
                xs[h, 17:20, at, :] = jnp.where(down, d, 0.0)[0:3]
    for o in (o0, o1, o2, o3):
        o[256:288] = p_ref[...]
    taps(sc, xs, kw_ref, True, sums, (o0, o1, o2, o3))


def conv_inner(sc, *args):
    o = jax.ShapeDtypeStruct((256, 256), BF)
    return pl.pallas_call(
        inner_kernel,
        out_shape=(o,) * 4,
        in_specs=[SM] + [VM] * 4,
        out_specs=(VM,) * 4,
        scratch_shapes=[pltpu.VMEM((2, 14, 144, 128), F32), pltpu.VMEM((4, 2, 256, 128), BF)],
        compiler_params=params(16),
        cost_estimate=pl.CostEstimate(flops=30_000_000, bytes_accessed=4 << 20, transcendentals=0),
        name="conv_inner",
    )(sc, *args)


def conv_edge(sc, *args):
    o = jax.ShapeDtypeStruct((288, 256), BF)
    return pl.pallas_call(
        edge_kernel,
        out_shape=(o,) * 4,
        in_specs=[SM] + [VM] * 7,
        out_specs=(VM,) * 4,
        scratch_shapes=[pltpu.VMEM((2, 20, 144, 128), F32), pltpu.VMEM((4, 2, 256, 128), BF)],
        compiler_params=params(16),
        cost_estimate=pl.CostEstimate(flops=30_000_000, bytes_accessed=4 << 20, transcendentals=0),
        name="conv_edge",
    )(sc, *args)


def gelu(p):
    return 0.5 * p * (1.0 + lax.erf(p * 0.7071067811865476))


def norm_kernel(sc, i0, i1, i2, i3, e0, e1, e2, e3, n_ref, bias):
    sides = []
    for k, (inner, edge) in enumerate(((i0, e0), (i1, e1), (i2, e2), (i3, e3))):
        p = sum(edge[256 + 8 * t : 264 + 8 * t, :].astype(F32) for t in (2, 1, 0))
        for i in range(8):
            bias[(4 - k) % 4, i] = p[3 + i // 2 : 4 + i // 2, i % 2 * 128 : i % 2 * 128 + 128]
        sides.append((inner, edge, p))
    for part in range(2):
        @pl.loop(0, 2)
        def _(step):
            rows = pl.ds(pl.multiple_of(step * 128, 128), 128)
            total = jnp.zeros((128, 1), F32)
            squares = jnp.zeros((128, 1), F32)
            for *m, p in sides:
                v = m[part][rows, :].astype(F32) + p[0:1]
                total = total + jnp.sum(v, axis=1, keepdims=True)
                squares = squares + jnp.sum(v * v, axis=1, keepdims=True)
            mean = total * (1.0 / 1024)
            rstd = lax.rsqrt(squares * (1.0 / 1024) - mean * mean + 1e-06)
            at = pl.ds(pl.multiple_of(256 * part + step * 128, 128), 128)
            for k, (*m, p) in enumerate(sides):
                q = lax.rem(sc[0] + 4 - k, 4)
                v = m[part][rows, :].astype(F32) + p[0:1]
                v = (v - mean) * rstd * p[1:2] + p[2:3]
                n_ref[at, pl.ds(pl.multiple_of(q * 256, 256), 256)] = v.astype(BF)


def norm(sc, inner, edge):
    return pl.pallas_call(
        norm_kernel,
        out_shape=(
            jax.ShapeDtypeStruct((512, 1024), BF),
            jax.ShapeDtypeStruct((4, 8, 1, 128), F32),
        ),
        in_specs=[SM] + [VM] * 8,
        out_specs=(VM, VM),
        compiler_params=params(16),
        cost_estimate=pl.CostEstimate(flops=1 << 23, bytes_accessed=2 << 20, transcendentals=0),
        name="norm",
    )(sc, *inner, *edge)


def hidden_block(n, win, wout, bias):
    pre = lax.dot_general(n, win, NT, preferred_element_type=F32)
    h = gelu(pre + bias).astype(BF)
    return jnp.dot(h, wout, preferred_element_type=F32)


def shards_bias(sc, bias, shift):
    color = jnp.where(sc[1] == 0, sc[2], sc[3])
    return [bias[k, sc[1] * 4 + lax.rem(color + shift, 4)] for k in (1, 2, 3)]


def first_kernel(sc, n_ref, n_other, bias, w_in, w_out, out):
    own = pl.ds(pl.multiple_of(sc[1] * 512, 512), 512)
    values = jnp.concatenate([bias[0, sc[1] * 4 + c] for c in range(4)], axis=1)

    @pl.loop(0, 2)
    def _(half):
        n = jnp.where(half == 0, n_ref[...], n_other[...])
        total = hidden_block(n, w_in[own, :], w_out[own, :], values)
        here = pl.ds(pl.multiple_of(half * 512, 512), 512)
        for q in range(4):
            out[q, here, :] = total[:, q * 256 : (q + 1) * 256]


def middle_kernel(
    sc, n_ref, n_other, bias, acc, held, plus, minus, out, win, wout, bv, sems
):
    pairs = []
    for at, size, w in ((0, 384, held), (384, 384, plus), (768, 256, minus)):
        pairs.append((w.at[0:size], win.at[at : at + size]))
        pairs.append((w.at[384 : 384 + size], wout.at[at : at + size]))
    copies = [pltpu.make_async_copy(a, b, sems.at[i]) for i, (a, b) in enumerate(pairs)]
    for copy in copies:
        copy.start()
    values = []
    for shift in (0, 1, 3):
        values += shards_bias(sc, bias, shift)
    for i in range(8):
        bv[i // 4, :, i % 4 * 128 : i % 4 * 128 + 128] = values[i]
    for copy in copies:
        copy.wait()

    @pl.loop(0, 4)
    def _(step):
        half, chunk = lax.rem(step, 2), step // 2
        rows = pl.ds(pl.multiple_of(chunk * 512, 512), 512)
        n = jnp.where(half == 0, n_ref[...], n_other[...])
        total = hidden_block(n, win[rows, :], wout[rows, :], bv[chunk])
        here = pl.ds(pl.multiple_of(half * 512, 512), 512)
        for q in range(4):
            before = jnp.where(step < 2, acc[q, here, :], out[q, here, :])
            out[q, here, :] = before + total[:, q * 256 : (q + 1) * 256]


def last_kernel(at, sc, n_ref, bias, acc, minus, low, high, out):
    win = jnp.concatenate([minus[256:384, :], low[...]])
    wout = jnp.concatenate([minus[640:768, :], high[...]])
    values = jnp.concatenate(shards_bias(sc, bias, 3)[2:] + shards_bias(sc, bias, 2), axis=1)
    total = hidden_block(n_ref[...], win, wout, values)
    for q in range(4):
        part = acc[q, at : at + 512, :] + total[:, q * 256 : (q + 1) * 256]
        out[q] = part.astype(out.dtype)


def mlp(kernel, sc, arrays, size, rows, out, name):
    middle = [
        pltpu.VMEM((1024, 1024), BF),
        pltpu.VMEM((1024, 1024), BF),
        pltpu.VMEM((2, 1, 512), F32),
        pltpu.SemaphoreType.DMA((6,)),
    ]
    return pl.pallas_call(
        kernel,
        out_shape=jax.ShapeDtypeStruct((4, rows, 256), out),
        in_specs=[SM] + [VM] * len(arrays),
        out_specs=VM,
        scratch_shapes=middle if size == 1024 else [],
        compiler_params=params(20),
        cost_estimate=pl.CostEstimate(
            flops=4_000 * size * rows, bytes_accessed=6 << 20, transcendentals=size * rows
        ),
        name=name,
    )(sc, *arrays)


def add_kernel(sc, acc, other, o0, o1, o2, o3):
    for k, o in enumerate((o0, o1, o2, o3)):
        q = lax.rem(sc[0] + k, 4)
        o[...] = (acc[q] + other[q].astype(F32)).astype(BF)


def add(sc, acc, other):
    return pl.pallas_call(
        add_kernel,
        out_shape=(jax.ShapeDtypeStruct((512, 256), BF),) * 4,
        in_specs=[SM, VM, VM],
        out_specs=(VM,) * 4,
        compiler_params=params(16),
        cost_estimate=pl.CostEstimate(flops=1 << 20, bytes_accessed=4 << 20, transcendentals=0),
        name="add",
    )(sc, acc, other)


def join_kernel(r1, ra, rb, r3, _, held, low, high, sems):
    moves = [(r1.at[0:128], 0), (ra, 128), (r3.at[0:128], 256)]
    moves += [(r1.at[128:256], 384), (rb, 512), (r3.at[128:256], 640)]
    copies = []
    for i, (src, at) in enumerate(moves):
        half, base = (low, at) if at < 384 else (high, at - 384)
        copies.append(pltpu.make_async_copy(src, held.at[at : at + 128], sems.at[2 * i]))
        copies.append(pltpu.make_async_copy(src, half.at[base : base + 128], sems.at[2 * i + 1]))
    for copy in copies:
        copy.start()
    for copy in copies:
        copy.wait()


def join(*pieces):
    half = jax.ShapeDtypeStruct((384, 1024), BF)
    return pl.pallas_call(
        join_kernel,
        out_shape=(jax.ShapeDtypeStruct((768, 1024), BF), half, half),
        in_specs=[HB] * 5,
        out_specs=(HB,) * 3,
        scratch_shapes=[pltpu.SemaphoreType.DMA((12,))],
        compiler_params=params(16),
        cost_estimate=pl.CostEstimate(flops=0, bytes_accessed=6 << 20, transcendentals=0),
        name="join",
    )(*pieces)


def spread_kernel(f, ls_ref, bo_ref, o_ref):
    for i in range(4):
        v = ls_ref[...] * (f[i * 128 : (i + 1) * 128, :].astype(F32) + bo_ref[...])
        for h in range(2):
            o_ref[i, h * 128 : (h + 1) * 128, :] = v[:, h * 128 : (h + 1) * 128].T


def spread(f, ls, bo):
    return pl.pallas_call(
        spread_kernel,
        out_shape=jax.ShapeDtypeStruct((4, 256, 128), F32),
        in_specs=[VM] * 3,
        out_specs=VM,
        compiler_params=params(16),
        cost_estimate=pl.CostEstimate(flops=1 << 18, bytes_accessed=1 << 20, transcendentals=0),
        name="spread",
    )(f, ls, bo)


def final_kernel(sc, x_ref, s0, s1, s2, s3, o_ref, t):
    for k, s in enumerate((s0, s1, s2, s3)):
        t[lax.rem(sc[0] + 4 - k, 4)] = s[...]
    order = ((0, 2), (1, 2), (0, 0), (1, 0), (2, 0), (3, 0), (2, 2), (3, 2))
    for c in range(0, 256, 8):
        v = jnp.concatenate([t[q, i : i + 2, c : c + 8, :] for q, i in order])
        v = jnp.swapaxes(v, 0, 1)
        o_ref[c : c + 8] = (x_ref[c : c + 8].astype(F32) + v).astype(BF)


def final(sc, x, parts):
    return pl.pallas_call(
        final_kernel,
        out_shape=jax.ShapeDtypeStruct((256, 16, 128), BF),
        in_specs=[SM] + [VM] * 5,
        out_specs=VM,
        scratch_shapes=[pltpu.VMEM((4, 4, 256, 128), F32)],
        compiler_params=params(16),
        cost_estimate=pl.CostEstimate(flops=1 << 20, bytes_accessed=4 << 20, transcendentals=0),
        name="final",
    )(sc, x, *parts)


def from_hid(x, k):
    return lax.ppermute(x, "hid", [((i + k) % 4, i) for i in range(4)])


def to_hid(x, k):
    return lax.ppermute(x, "hid", [(i, (i + k) % 4) for i in range(4)])


def place(x, z, core):
    return (x * 4 + z % 4) * 4 + (z // 4) * 2 + core


def from_plane(v, step, major):
    pairs = []
    for x in range(4):
        for z in range(8):
            for core in range(2):
                along_x = (core == 0) == major
                sx, sz = ((x + step) % 4, z) if along_x else (x, (z + step) % 8)
                pairs.append((place(sx, sz, core), place(x, z, core)))
    return lax.ppermute(v, ("row", "col"), pairs)


def from_core(v):
    return lax.ppermute(v, "col", [(0, 1), (1, 0), (2, 3), (3, 2)])


def around(v, up):
    return lax.ppermute(v, "row", [(i, (i + (1 if up else -1)) % 16) for i in range(16)])


def from_chip(v):
    return lax.ppermute(v, "col", [(1, 2), (2, 1), (0, 3), (3, 0)])


def after(values, *others):
    values = tuple(values)
    return lax.optimization_barrier(values + others)[: len(values)]


def on_device(
    features, dw_kernel, dw_bias, norm_gain, norm_bias, w_in, b_in, w_out, b_out, layer_scale
):
    row, col, y = lax.axis_index("row"), lax.axis_index("col"), lax.axis_index("hid")
    x, zl, core = row // 4, row % 4, col % 2
    c0, c1 = (x + 2 * zl) % 4, (2 * x + zl) % 4
    color = jnp.where(core == 0, c0, c1)
    start = 512 * core + 128 * color
    sc = jnp.stack([y, core, c0, c1, row, 15 - row, col, 3 - col, start]).astype(jnp.int32)

    piece = jnp.concatenate(
        [
            lax.dynamic_slice_in_dim(w_in, start, 128, 0),
            lax.dynamic_slice_in_dim(w_out, start, 128, 0),
        ]
    )
    r1, r3 = from_hid(piece, 1), from_hid(piece, 3)

    xt, send_a, send_b = turn(sc, features)
    a, b = from_core(send_a), from_chip(send_b)
    kw = jnp.transpose(dw_kernel.reshape(2, 128, 49), (0, 2, 1))
    small = jnp.concatenate([dw_bias, norm_gain, norm_bias, b_in]).reshape(7, 256)
    small = jnp.pad(small, ((0, 1), (0, 0)))
    high = lax.reduce_precision(small, 8, 7)
    middle = lax.reduce_precision(small - high, 8, 7)
    lowest = small - high - middle
    small = jnp.concatenate([high, middle, lowest, jnp.zeros_like(high)]).astype(BF)
    b, kw, small = after([b, kw, small])
    down, up, ra, rb = pack(xt, a, b, r1, r3)
    top, bot = around(down, True), around(up, False)
    ra, rb = from_hid(ra, 1), from_hid(rb, 3)

    inner = conv_inner(sc, xt, a, b, kw)
    first = inner[0]
    inner = [inner[0]] + [to_hid(inner[k], k) for k in (1, 2, 3)]
    held, low, high = join(r1, ra, rb, r3, first)
    plane = [
        from_plane(held, 1, True),
        from_plane(held, -1, True),
        from_plane(low, 1, False),
        from_plane(high, -1, False),
    ]
    top, bot = after([top, bot], held)
    edge = conv_edge(sc, xt, a, b, top, bot, kw, small)
    edge = [edge[0]] + [to_hid(edge[k], k) for k in (1, 2, 3)]

    n, bias = norm(sc, inner, edge)
    n_other = from_core(n)
    plus, minus, low, high = plane
    acc = mlp(first_kernel, sc, [n, n_other, bias, w_in, w_out], 512, 1024, F32, "mlp_first")
    plus, minus, acc = after([plus, minus, acc])
    arrays = [n, n_other, bias, acc, held, plus, minus]
    acc = mlp(middle_kernel, sc, arrays, 1024, 1024, F32, "mlp_mid")
    low, high, acc = after([low, high, acc])
    last = functools.partial(last_kernel, 512)
    arrays = [bias, acc, minus, low, high]
    other = mlp(last, sc, [n_other] + arrays, 512, 512, BF, "mlp_last_other")
    back = from_core(other)
    (acc,) = after([acc], other)
    last = functools.partial(last_kernel, 0)
    arrays = [bias, acc, minus, low, high]
    acc = mlp(last, sc, [n] + arrays, 512, 512, F32, "mlp_last")
    parts = add(sc, acc, back)
    two, one, three = (to_hid(parts[k], k) for k in (2, 1, 3))
    ls, bo = layer_scale[None, :], b_out[None, :]
    parts = [spread(f, ls, bo) for f in (parts[0], one, two, three)]
    return final(sc, features, parts)


def solution(mesh):
    return jax.shard_map(
        on_device,
        mesh=mesh,
        in_specs=(
            P("hid", "row", "col"),
            P("hid", None, None),
            P("hid"),
            P("hid"),
            P("hid"),
            P("hid", None),
            P("hid"),
            P("hid", None),
            P("hid"),
            P("hid"),
        ),
        out_specs=P("hid", "row", "col"),
        check_vma=False,
    )
```

```python
import functools
import jax
import jax.numpy as jnp
from jax import lax
from jax.experimental import pallas as pl
from jax.experimental.pallas import tpu as pltpu
from jax.sharding import PartitionSpec as P

F32 = jnp.float32
BF = jnp.bfloat16
VM = pl.BlockSpec(memory_space=pltpu.VMEM)
SM = pl.BlockSpec(memory_space=pltpu.SMEM)
HB = pl.BlockSpec(memory_space=pl.ANY)
NT = (((1,), (1,)), ((), ()))
CB = 64


def params(mib):
    return pltpu.CompilerParams(vmem_limit_bytes=mib << 20)


def turn_kernel(sc, x_ref, xt_ref, a_ref, b_ref, xf):
    xf.reshape(256, 24, 128)[:, 0:16, :] = x_ref[...].astype(F32)
    for r in range(16):
        for h in range(2):
            t = xf[pl.ds(h * 3072 + r, 128, stride=24), :]
            xt_ref[r, :, h * 128 : (h + 1) * 128] = t.T.astype(BF)
    for j in range(3):
        js = slice(j * 256, (j + 1) * 256)
        low, high = xt_ref[:, j, :].astype(F32), xt_ref[:, 125 + j, :].astype(F32)
        a_ref[:, js] = jnp.where(sc[1] == 0, high, low).astype(BF)
        b_ref[:, js] = jnp.where(sc[1] == 0, low, high).astype(BF)


def turn(sc, x):
    edge = jax.ShapeDtypeStruct((16, 768), BF)
    return pl.pallas_call(
        turn_kernel,
        out_shape=(jax.ShapeDtypeStruct((16, 128, 256), BF), edge, edge),
        in_specs=[SM, VM],
        out_specs=(VM, VM, VM),
        scratch_shapes=[pltpu.VMEM((6144, 128), F32)],
        compiler_params=params(16),
        cost_estimate=pl.CostEstimate(flops=0, bytes_accessed=4 << 20, transcendentals=0),
        name="turn",
    )(sc, x)


def pack_kernel(xt_ref, a_ref, b_ref, r1_ref, r3_ref, down_ref, up_ref, relay_up, relay_down):
    for r in range(3):
        down_ref[r * 128 : (r + 1) * 128, :] = xt_ref[13 + r]
        up_ref[r * 128 : (r + 1) * 128, :] = xt_ref[r]
    edges = [
        edge[:, j * 256 : (j + 1) * 256].astype(F32) for edge in (a_ref, b_ref) for j in range(3)
    ]
    none = jnp.zeros((8, 256), F32)
    down_ref[384:416, :] = jnp.concatenate([v[12:16] for v in edges] + [none]).astype(BF)
    up_ref[384:416, :] = jnp.concatenate([v[0:4] for v in edges] + [none]).astype(BF)
    relay_up[...] = r1_ref[0:128, :]
    relay_down[...] = r3_ref[128:256, :]


def pack(xt, a, b, r1, r3):
    o = jax.ShapeDtypeStruct((416, 256), BF)
    w = jax.ShapeDtypeStruct((128, 1024), BF)
    return pl.pallas_call(
        pack_kernel,
        out_shape=(o, o, w, w),
        in_specs=[VM] * 5,
        out_specs=(VM,) * 4,
        compiler_params=params(16),
        cost_estimate=pl.CostEstimate(flops=0, bytes_accessed=2 << 20, transcendentals=0),
        name="pack",
    )(xt, a, b, r1, r3)


def taps(sc, xs, kw_ref, edge, sums, outs):
    @pl.loop(0, 4)
    def _(step):
        h, g = lax.rem(step, 2), step // 2
        row0 = (10 if edge else 4) * g
        for c0 in range(0, 128, CB):
            acc = [jnp.zeros((CB, 128), F32) for _ in range(4)]
            for b in range(7):
                for ri in range(10):
                    xv = xs[h, row0 + ri, c0 + 5 + b : c0 + 5 + b + CB, :]
                    for ro in range(4):
                        a = ri - ro
                        if 0 <= a < 7:
                            acc[ro] = acc[ro] + kw_ref[h, a * 7 + b : a * 7 + b + 1, :] * xv
            for ro in range(4):
                at = ro % 2 * 128 + c0
                sums[2 * g + ro // 2, h, at : at + CB, :] = acc[ro].astype(BF)

    for k, o in enumerate(outs):
        q = lax.rem(sc[0] + k, 4)
        for h in range(2):
            o[0:256, h * 128 : (h + 1) * 128] = sums[q, h]


def columns(sc, a, b):
    a, b, first = a.astype(F32), b.astype(F32), sc[1] == 0
    low = jnp.where(sc[6] > 0, jnp.where(first, b, a), 0.0)
    high = jnp.where(sc[7] > 0, jnp.where(first, a, b), 0.0)
    return low, high


def inner_kernel(sc, xt_ref, a_ref, b_ref, kw_ref, o0, o1, o2, o3, xs, sums):
    for h in range(2):
        hs = slice(h * 128, (h + 1) * 128)
        for r in range(14):
            xs[h, r, 8:136, :] = xt_ref[1 + r, :, hs].astype(F32)
        for j in range(3):
            js = slice(j * 256 + h * 128, j * 256 + (h + 1) * 128)
            low, high = columns(sc, a_ref[:, js], b_ref[:, js])
            xs[h, :, 5 + j, :] = low[1:15]
            xs[h, :, 136 + j, :] = high[1:15]
    taps(sc, xs, kw_ref, False, sums, (o0, o1, o2, o3))


def edge_kernel(
    sc, xt_ref, a_ref, b_ref, top_ref, bot_ref, kw_ref, p_ref, o0, o1, o2, o3, xs, sums
):
    up, down = sc[4] > 0, sc[5] > 0
    for h in range(2):
        hs = slice(h * 128, (h + 1) * 128)
        for r in range(7):
            xs[h, 3 + r, 8:136, :] = xt_ref[r, :, hs].astype(F32)
            xs[h, 10 + r, 8:136, :] = xt_ref[9 + r, :, hs].astype(F32)
        for r in range(3):
            rs = slice(r * 128, (r + 1) * 128)
            xs[h, r, 8:136, :] = jnp.where(up, top_ref[rs, hs].astype(F32), 0.0)
            xs[h, 17 + r, 8:136, :] = jnp.where(down, bot_ref[rs, hs].astype(F32), 0.0)
        tc, bc = top_ref[384:416, hs].astype(F32), bot_ref[384:416, hs].astype(F32)
        for j in range(3):
            js = slice(j * 256 + h * 128, j * 256 + (h + 1) * 128)
            sides = columns(sc, a_ref[:, js], b_ref[:, js])
            ra, rb = slice(4 * j, 4 * j + 4), slice(12 + 4 * j, 16 + 4 * j)
            tops = columns(sc, tc[ra], tc[rb])
            bots = columns(sc, bc[ra], bc[rb])
            for at, v, t, d in zip((5 + j, 136 + j), sides, tops, bots):
                xs[h, 3:10, at, :] = v[0:7]
                xs[h, 10:17, at, :] = v[9:16]
                xs[h, 0:3, at, :] = jnp.where(up, t, 0.0)[1:4]
                xs[h, 17:20, at, :] = jnp.where(down, d, 0.0)[0:3]
    for o in (o0, o1, o2, o3):
        o[256:288] = p_ref[...]
    taps(sc, xs, kw_ref, True, sums, (o0, o1, o2, o3))


def conv_inner(sc, *args):
    o = jax.ShapeDtypeStruct((256, 256), BF)
    return pl.pallas_call(
        inner_kernel,
        out_shape=(o,) * 4,
        in_specs=[SM] + [VM] * 4,
        out_specs=(VM,) * 4,
        scratch_shapes=[pltpu.VMEM((2, 14, 144, 128), F32), pltpu.VMEM((4, 2, 256, 128), BF)],
        compiler_params=params(16),
        cost_estimate=pl.CostEstimate(flops=30_000_000, bytes_accessed=4 << 20, transcendentals=0),
        name="conv_inner",
    )(sc, *args)


def conv_edge(sc, *args):
    o = jax.ShapeDtypeStruct((288, 256), BF)
    return pl.pallas_call(
        edge_kernel,
        out_shape=(o,) * 4,
        in_specs=[SM] + [VM] * 7,
        out_specs=(VM,) * 4,
        scratch_shapes=[pltpu.VMEM((2, 20, 144, 128), F32), pltpu.VMEM((4, 2, 256, 128), BF)],
        compiler_params=params(16),
        cost_estimate=pl.CostEstimate(flops=30_000_000, bytes_accessed=4 << 20, transcendentals=0),
        name="conv_edge",
    )(sc, *args)


def gelu(p):
    return 0.5 * p * (1.0 + lax.erf(p * 0.7071067811865476))


def norm_kernel(sc, i0, i1, i2, i3, e0, e1, e2, e3, n_ref, bias):
    sides = []
    for k, (inner, edge) in enumerate(((i0, e0), (i1, e1), (i2, e2), (i3, e3))):
        p = sum(edge[256 + 8 * t : 264 + 8 * t, :].astype(F32) for t in (2, 1, 0))
        for i in range(8):
            bias[(4 - k) % 4, i] = p[3 + i // 2 : 4 + i // 2, i % 2 * 128 : i % 2 * 128 + 128]
        sides.append((inner, edge, p))
    for part in range(2):
        @pl.loop(0, 2)
        def _(step):
            rows = pl.ds(pl.multiple_of(step * 128, 128), 128)
            total = jnp.zeros((128, 1), F32)
            squares = jnp.zeros((128, 1), F32)
            for *m, p in sides:
                v = m[part][rows, :].astype(F32) + p[0:1]
                total = total + jnp.sum(v, axis=1, keepdims=True)
                squares = squares + jnp.sum(v * v, axis=1, keepdims=True)
            mean = total * (1.0 / 1024)
            rstd = lax.rsqrt(squares * (1.0 / 1024) - mean * mean + 1e-06)
            at = pl.ds(pl.multiple_of(256 * part + step * 128, 128), 128)
            for k, (*m, p) in enumerate(sides):
                q = lax.rem(sc[0] + 4 - k, 4)
                v = m[part][rows, :].astype(F32) + p[0:1]
                v = (v - mean) * rstd * p[1:2] + p[2:3]
                n_ref[at, pl.ds(pl.multiple_of(q * 256, 256), 256)] = v.astype(BF)


def norm(sc, inner, edge):
    return pl.pallas_call(
        norm_kernel,
        out_shape=(
            jax.ShapeDtypeStruct((512, 1024), BF),
            jax.ShapeDtypeStruct((4, 8, 1, 128), F32),
        ),
        in_specs=[SM] + [VM] * 8,
        out_specs=(VM, VM),
        compiler_params=params(16),
        cost_estimate=pl.CostEstimate(flops=1 << 23, bytes_accessed=2 << 20, transcendentals=0),
        name="norm",
    )(sc, *inner, *edge)


def hidden_block(n, win, wout, bias):
    pre = lax.dot_general(n, win, NT, preferred_element_type=F32)
    h = gelu(pre + bias).astype(BF)
    return jnp.dot(h, wout, preferred_element_type=F32)


def shards_bias(sc, bias, shift):
    color = jnp.where(sc[1] == 0, sc[2], sc[3])
    return [bias[k, sc[1] * 4 + lax.rem(color + shift, 4)] for k in (1, 2, 3)]


def first_kernel(sc, n_ref, n_other, bias, w_in, w_out, out):
    own = pl.ds(pl.multiple_of(sc[1] * 512, 512), 512)
    values = jnp.concatenate([bias[0, sc[1] * 4 + c] for c in range(4)], axis=1)

    @pl.loop(0, 2)
    def _(half):
        n = jnp.where(half == 0, n_ref[...], n_other[...])
        total = hidden_block(n, w_in[own, :], w_out[own, :], values)
        here = pl.ds(pl.multiple_of(half * 512, 512), 512)
        for q in range(4):
            out[q, here, :] = total[:, q * 256 : (q + 1) * 256]


def middle_kernel(
    sc, n_ref, n_other, bias, acc, held, plus, minus, out, win, wout, bv, sems
):
    pairs = []
    for at, size, w in ((0, 384, held), (384, 384, plus), (768, 256, minus)):
        pairs.append((w.at[0:size], win.at[at : at + size]))
        pairs.append((w.at[384 : 384 + size], wout.at[at : at + size]))
    copies = [pltpu.make_async_copy(a, b, sems.at[i]) for i, (a, b) in enumerate(pairs)]
    for copy in copies:
        copy.start()
    values = []
    for shift in (0, 1, 3):
        values += shards_bias(sc, bias, shift)
    for i in range(8):
        bv[i // 4, :, i % 4 * 128 : i % 4 * 128 + 128] = values[i]
    for copy in copies[:4]:
        copy.wait()

    @pl.loop(0, 4)
    def _(step):
        @pl.when(step == 2)
        def _():
            for copy in copies[4:]:
                copy.wait()

        half, chunk = lax.rem(step, 2), step // 2
        rows = pl.ds(pl.multiple_of(chunk * 512, 512), 512)
        n = jnp.where(half == 0, n_ref[...], n_other[...])
        total = hidden_block(n, win[rows, :], wout[rows, :], bv[chunk])
        here = pl.ds(pl.multiple_of(half * 512, 512), 512)
        for q in range(4):
            before = jnp.where(step < 2, acc[q, here, :], out[q, here, :])
            out[q, here, :] = before + total[:, q * 256 : (q + 1) * 256]


def last_kernel(at, sc, n_ref, bias, acc, minus, low, high, out):
    win = jnp.concatenate([minus[256:384, :], low[...]])
    wout = jnp.concatenate([minus[640:768, :], high[...]])
    values = jnp.concatenate(shards_bias(sc, bias, 3)[2:] + shards_bias(sc, bias, 2), axis=1)
    total = hidden_block(n_ref[...], win, wout, values)
    for q in range(4):
        part = acc[q, at : at + 512, :] + total[:, q * 256 : (q + 1) * 256]
        out[q] = part.astype(out.dtype)


def mlp(kernel, sc, arrays, size, rows, out, name):
    middle = [
        pltpu.VMEM((1024, 1024), BF),
        pltpu.VMEM((1024, 1024), BF),
        pltpu.VMEM((2, 1, 512), F32),
        pltpu.SemaphoreType.DMA((6,)),
    ]
    return pl.pallas_call(
        kernel,
        out_shape=jax.ShapeDtypeStruct((4, rows, 256), out),
        in_specs=[SM] + [VM] * len(arrays),
        out_specs=VM,
        scratch_shapes=middle if size == 1024 else [],
        compiler_params=params(20),
        cost_estimate=pl.CostEstimate(
            flops=4_000 * size * rows, bytes_accessed=6 << 20, transcendentals=size * rows
        ),
        name=name,
    )(sc, *arrays)


def add_kernel(sc, acc, other, o0, o1, o2, o3):
    for k, o in enumerate((o0, o1, o2, o3)):
        q = lax.rem(sc[0] + k, 4)
        o[...] = (acc[q] + other[q].astype(F32)).astype(BF)


def add(sc, acc, other):
    return pl.pallas_call(
        add_kernel,
        out_shape=(jax.ShapeDtypeStruct((512, 256), BF),) * 4,
        in_specs=[SM, VM, VM],
        out_specs=(VM,) * 4,
        compiler_params=params(16),
        cost_estimate=pl.CostEstimate(flops=1 << 20, bytes_accessed=4 << 20, transcendentals=0),
        name="add",
    )(sc, acc, other)


def join_kernel(r1, ra, rb, r3, _, held, low, high, sems):
    moves = [(r1.at[0:128], 0), (ra, 128), (r3.at[0:128], 256)]
    moves += [(r1.at[128:256], 384), (rb, 512), (r3.at[128:256], 640)]
    copies = []
    for i, (src, at) in enumerate(moves):
        half, base = (low, at) if at < 384 else (high, at - 384)
        copies.append(pltpu.make_async_copy(src, held.at[at : at + 128], sems.at[2 * i]))
        copies.append(pltpu.make_async_copy(src, half.at[base : base + 128], sems.at[2 * i + 1]))
    for copy in copies:
        copy.start()
    for copy in copies:
        copy.wait()


def join(*pieces):
    half = jax.ShapeDtypeStruct((384, 1024), BF)
    return pl.pallas_call(
        join_kernel,
        out_shape=(jax.ShapeDtypeStruct((768, 1024), BF), half, half),
        in_specs=[HB] * 5,
        out_specs=(HB,) * 3,
        scratch_shapes=[pltpu.SemaphoreType.DMA((12,))],
        compiler_params=params(16),
        cost_estimate=pl.CostEstimate(flops=0, bytes_accessed=6 << 20, transcendentals=0),
        name="join",
    )(*pieces)


def spread_kernel(f, ls_ref, bo_ref, o_ref):
    for i in range(4):
        v = ls_ref[...] * (f[i * 128 : (i + 1) * 128, :].astype(F32) + bo_ref[...])
        for h in range(2):
            o_ref[i, h * 128 : (h + 1) * 128, :] = v[:, h * 128 : (h + 1) * 128].T


def spread(f, ls, bo):
    return pl.pallas_call(
        spread_kernel,
        out_shape=jax.ShapeDtypeStruct((4, 256, 128), F32),
        in_specs=[VM] * 3,
        out_specs=VM,
        compiler_params=params(16),
        cost_estimate=pl.CostEstimate(flops=1 << 18, bytes_accessed=1 << 20, transcendentals=0),
        name="spread",
    )(f, ls, bo)


def final_kernel(sc, x_ref, s0, s1, s2, s3, o_ref, t):
    for k, s in enumerate((s0, s1, s2, s3)):
        t[lax.rem(sc[0] + 4 - k, 4)] = s[...]
    order = ((0, 2), (1, 2), (0, 0), (1, 0), (2, 0), (3, 0), (2, 2), (3, 2))
    for c in range(0, 256, 8):
        v = jnp.concatenate([t[q, i : i + 2, c : c + 8, :] for q, i in order])
        v = jnp.swapaxes(v, 0, 1)
        o_ref[c : c + 8] = (x_ref[c : c + 8].astype(F32) + v).astype(BF)


def final(sc, x, parts):
    return pl.pallas_call(
        final_kernel,
        out_shape=jax.ShapeDtypeStruct((256, 16, 128), BF),
        in_specs=[SM] + [VM] * 5,
        out_specs=VM,
        scratch_shapes=[pltpu.VMEM((4, 4, 256, 128), F32)],
        compiler_params=params(16),
        cost_estimate=pl.CostEstimate(flops=1 << 20, bytes_accessed=4 << 20, transcendentals=0),
        name="final",
    )(sc, x, *parts)


def from_hid(x, k):
    return lax.ppermute(x, "hid", [((i + k) % 4, i) for i in range(4)])


def to_hid(x, k):
    return lax.ppermute(x, "hid", [(i, (i + k) % 4) for i in range(4)])


def place(x, z, core):
    return (x * 4 + z % 4) * 4 + (z // 4) * 2 + core


def from_plane(v, step, major):
    pairs = []
    for x in range(4):
        for z in range(8):
            for core in range(2):
                along_x = (core == 0) == major
                sx, sz = ((x + step) % 4, z) if along_x else (x, (z + step) % 8)
                pairs.append((place(sx, sz, core), place(x, z, core)))
    return lax.ppermute(v, ("row", "col"), pairs)


def from_core(v):
    return lax.ppermute(v, "col", [(0, 1), (1, 0), (2, 3), (3, 2)])


def around(v, up):
    return lax.ppermute(v, "row", [(i, (i + (1 if up else -1)) % 16) for i in range(16)])


def from_chip(v):
    return lax.ppermute(v, "col", [(1, 2), (2, 1), (0, 3), (3, 0)])


def after(values, *others):
    values = tuple(values)
    return lax.optimization_barrier(values + others)[: len(values)]


def on_device(
    features, dw_kernel, dw_bias, norm_gain, norm_bias, w_in, b_in, w_out, b_out, layer_scale
):
    row, col, y = lax.axis_index("row"), lax.axis_index("col"), lax.axis_index("hid")
    x, zl, core = row // 4, row % 4, col % 2
    c0, c1 = (x + 2 * zl) % 4, (2 * x + zl) % 4
    color = jnp.where(core == 0, c0, c1)
    start = 512 * core + 128 * color
    sc = jnp.stack([y, core, c0, c1, row, 15 - row, col, 3 - col, start]).astype(jnp.int32)

    piece = jnp.concatenate(
        [
            lax.dynamic_slice_in_dim(w_in, start, 128, 0),
            lax.dynamic_slice_in_dim(w_out, start, 128, 0),
        ]
    )
    r1, r3 = from_hid(piece, 1), from_hid(piece, 3)

    xt, send_a, send_b = turn(sc, features)
    a, b = from_core(send_a), from_chip(send_b)
    kw = jnp.transpose(dw_kernel.reshape(2, 128, 49), (0, 2, 1))
    small = jnp.concatenate([dw_bias, norm_gain, norm_bias, b_in]).reshape(7, 256)
    small = jnp.pad(small, ((0, 1), (0, 0)))
    high = lax.reduce_precision(small, 8, 7)
    middle = lax.reduce_precision(small - high, 8, 7)
    lowest = small - high - middle
    small = jnp.concatenate([high, middle, lowest, jnp.zeros_like(high)]).astype(BF)
    b, kw, small = after([b, kw, small])
    down, up, ra, rb = pack(xt, a, b, r1, r3)
    top, bot = around(down, True), around(up, False)
    ra, rb = from_hid(ra, 1), from_hid(rb, 3)

    inner = conv_inner(sc, xt, a, b, kw)
    first = inner[0]
    inner = [inner[0]] + [to_hid(inner[k], k) for k in (1, 2, 3)]
    held, low, high = join(r1, ra, rb, r3, first)
    plane = [
        from_plane(held, 1, True),
        from_plane(held, -1, True),
        from_plane(low, 1, False),
        from_plane(high, -1, False),
    ]
    top, bot = after([top, bot], held)
    edge = conv_edge(sc, xt, a, b, top, bot, kw, small)
    edge = [edge[0]] + [to_hid(edge[k], k) for k in (1, 2, 3)]

    n, bias = norm(sc, inner, edge)
    n_other = from_core(n)
    plus, minus, low, high = plane
    acc = mlp(first_kernel, sc, [n, n_other, bias, w_in, w_out], 512, 1024, F32, "mlp_first")
    plus, minus, acc = after([plus, minus, acc])
    arrays = [n, n_other, bias, acc, held, plus, minus]
    acc = mlp(middle_kernel, sc, arrays, 1024, 1024, F32, "mlp_mid")
    low, high, acc = after([low, high, acc])
    last = functools.partial(last_kernel, 512)
    arrays = [bias, acc, minus, low, high]
    other = mlp(last, sc, [n_other] + arrays, 512, 512, BF, "mlp_last_other")
    back = from_core(other)
    (acc,) = after([acc], other)
    last = functools.partial(last_kernel, 0)
    arrays = [bias, acc, minus, low, high]
    acc = mlp(last, sc, [n] + arrays, 512, 512, F32, "mlp_last")
    parts = add(sc, acc, back)
    two, one, three = (to_hid(parts[k], k) for k in (2, 1, 3))
    ls, bo = layer_scale[None, :], b_out[None, :]
    parts = [spread(f, ls, bo) for f in (parts[0], one, two, three)]
    return final(sc, features, parts)


def solution(mesh):
    return jax.shard_map(
        on_device,
        mesh=mesh,
        in_specs=(
            P("hid", "row", "col"),
            P("hid", None, None),
            P("hid"),
            P("hid"),
            P("hid"),
            P("hid", None),
            P("hid"),
            P("hid", None),
            P("hid"),
            P("hid"),
        ),
        out_specs=P("hid", "row", "col"),
        check_vma=False,
    )
```
